32 devices in a mesh: groups: 2 (over y), expert: 4 (over z), tensor: 4 (over x, core).
Axes of the slice: x: 2, y: 2, z: 4, core: 2. Of those that a mesh axis runs over, the one named last changes fastest.
Arguments:
- tokens: bfloat16 [256, 3072], P(('groups', 'expert'), 'tensor'), parts along dimension 0, may hold values from -6 to 6
- cotangent: bfloat16 [256, 3072], P(('groups', 'expert'), 'tensor'), parts along dimension 0, may hold values from -6 to 6
- route_weights: float32 [256, 2], P(('groups', 'expert')), parts along dimension 0, may hold values from 0.2 to 1
- expert_ids: int32 [256, 2], P(('groups', 'expert')), parts along dimension 0, may hold values from 0 to 3, as said below
- slot_index: int32 [256, 2], P(('groups', 'expert')), parts along dimension 0, may hold values from 0 to 15, as said below
- keep_mask: int32 [256, 2], P(('groups', 'expert')), parts along dimension 0, may hold values from 0 to 1, as said below
- w_gate: bfloat16 [3072, 32768], P(None, ('expert', 'tensor')), may hold values from -0.109375 to 0.109375
- w_up: bfloat16 [3072, 32768], P(None, ('expert', 'tensor')), may hold values from -0.109375 to 0.109375
- w_down: bfloat16 [32768, 3072], P(('expert', 'tensor')), may hold values from -0.0625 to 0.0625
Outputs:
- grad_tokens: bfloat16 [256, 3072], P(('groups', 'expert'), 'tensor'), parts along dimension 0
- grad_down: bfloat16 [65536, 3072], P(('groups', 'expert', 'tensor')), parts along dimension 0
The draws below stay inside these ranges and needn't reach their ends.
There are 2 independent parts, one for each index of `groups`. The reference program is written for one: setup_inputs(seed, part) draws one part's arguments, and reference() takes and returns one part's arrays. A program takes and returns all parts, laid end to end along the dimension named above; an argument that names none is the same for every part. Nothing has to cross between parts.
Inputs may be any that keep to these rules, and one draw needn't show every extreme that they name: `expert_ids`: the two experts of a token differ. `slot_index`: within the 32 rows of one index of expert, the assignments to one expert are numbered 0, 1, 2, ... in the order of tokens and then of k; the number is given where it is under 16, else 16 - 1. `keep_mask`: 1 exactly where the assignment's number within its aligned block of 32 rows is under 16; in every block some expert is full.
All inputs are finite; a program needn't handle non-finite values.
Results may differ from the reference program's by a relative error of at most 0.012.
Values may be sent and summed in bfloat16 or wider, within the bound.
A program may use at most 128 MiB of HBM per device.

```python
import jax
import jax.numpy as jnp
from jax import lax

D = 3072
FF = 8192
EXPERTS = 4
TOK_DEV = 32
CAP = 16
GROUP = 1
FF_DEV = 2048
TOKENS = 128
N_EXPERT = 4
N_TENSOR = 4


def route_table(key):
    hot_key, block_key, score_key, pick_key = jax.random.split(key, 4)
    blocks = TOKENS // TOK_DEV
    base = jax.random.randint(score_key, (blocks, TOK_DEV, EXPERTS), 0, 1 << 20)
    column_position = jnp.arange(EXPERTS, dtype=jnp.int32)[None, None, :]
    router_logits = base * EXPERTS + column_position
    selection_matrix_full = jax.random.randint(hot_key, (), 0, EXPERTS)
    selection_matrix_block = jax.random.randint(block_key, (blocks, 1, 1), 0, EXPERTS)
    order = jax.vmap(lambda sub: jax.random.permutation(sub, TOK_DEV))(jax.random.split(pick_key, blocks))
    selected_expert = (order % 4)[:, :, None]
    extra_score = jnp.where((column_position == selection_matrix_full) & (selected_expert == 0), 1 << 28, 0)
    extra_score = extra_score + jnp.where((column_position == selection_matrix_block) & (selected_expert == 1), 1 << 28, 0)
    router_logits = router_logits + extra_score.astype(jnp.int32)
    chosen = lax.top_k(router_logits, 2)[1].astype(jnp.int32)
    flat_ids = chosen.reshape(blocks, TOK_DEV * 2)
    onehot = (flat_ids[:, :, None] == jnp.arange(EXPERTS, dtype=jnp.int32)[None, None, :]).astype(jnp.int32)
    before = jnp.cumsum(onehot, axis=1) - onehot
    number = jnp.sum(before * onehot, axis=2)
    keep = (number < CAP).astype(jnp.int32)
    slot = jnp.minimum(number, CAP - 1).astype(jnp.int32)
    return (chosen.reshape(TOKENS, 2), slot.reshape(TOKENS, 2), keep.reshape(TOKENS, 2))


def draw_expert_ids(key, part):
    return route_table(key)[0]


def draw_slot_index(key, part):
    return route_table(key)[1]


def draw_keep_mask(key, part):
    return route_table(key)[2]


def levels(rng, dims, shards, low, largest):
    level, own = 1.0, jax.random.fold_in(rng, 6)
    for dim, shards_of in shards:
        draws = jnp.exp(jax.random.uniform(jax.random.fold_in(own, dim), (shards_of,), jnp.float32, low / len(shards), largest / len(shards)))
        level = level * jnp.repeat(draws, dims[dim] // shards_of).reshape([-1 if axis == dim else 1 for axis in range(len(dims))])
    return level


def centred(rng, extent, scale, reach, shards=(), kind=jnp.bfloat16):
    entries = jax.random.normal(rng, extent, jnp.float32) * scale
    if len(shards) > 0:
        entries = levels(rng, extent, shards, -0.22, 0.18) * entries
    return jnp.clip(entries, min=-reach, max=reach).astype(kind)


def setup_inputs(seed: int = 0, part: int = 0) -> dict:
    arg_keys = jax.random.split(jax.random.key(seed), 10)
    part_splits = jax.random.split(jax.random.fold_in(arg_keys[9], part), 10)
    return {
        "tokens": centred(part_splits[0], (TOKENS, D), 1.0, 6.0, ((0, 4), (1, 4))),
        "cotangent": centred(part_splits[1], (TOKENS, D), 1.0, 6.0, ((0, 4), (1, 4))),
        "route_weights": jnp.clip(0.2 + 0.8 * jax.random.uniform(part_splits[2], (TOKENS, 2), jnp.float32) ** levels(part_splits[2], (TOKENS, 2), ((0, 4),), -0.2, 0.2), 0.2, 1.0),
        "expert_ids": draw_expert_ids(jax.random.fold_in(jax.random.fold_in(arg_keys[9], part), 71), part),
        "slot_index": draw_slot_index(jax.random.fold_in(jax.random.fold_in(arg_keys[9], part), 71), part),
        "keep_mask": draw_keep_mask(jax.random.fold_in(jax.random.fold_in(arg_keys[9], part), 71), part),
        "w_gate": centred(arg_keys[6], (D, EXPERTS * FF), D ** -0.5, 0.109375, ((1, 16),)),
        "w_up": centred(arg_keys[7], (D, EXPERTS * FF), D ** -0.5, 0.109375, ((1, 16),)),
        "w_down": centred(arg_keys[8], (EXPERTS * FF, D), FF ** -0.5, 0.0625, ((0, 16),)),
    }


def reference(tokens, cotangent, route_weights, expert_ids, slot_index, keep_mask, w_gate, w_up, w_down):
    rows_all = N_EXPERT * CAP
    dump_row = EXPERTS * rows_all
    blocks = GROUP * N_TENSOR
    source = (jnp.arange(TOKENS, dtype=jnp.int32) // TOK_DEV).astype(jnp.int32)
    target = expert_ids * rows_all + source[:, None] * CAP + slot_index
    target = jnp.where(keep_mask == 1, target, dump_row).reshape(-1).astype(jnp.int32)
    owners = jnp.full((dump_row + 1,), 2 * TOKENS, jnp.int32)
    owners = owners.at[target].set(jnp.arange(2 * TOKENS, dtype=jnp.int32))
    owners = owners[:dump_row].reshape(EXPERTS, rows_all)
    token_ext = jnp.concatenate([tokens, jnp.zeros((1, D), tokens.dtype)], axis=0)
    weighted = (route_weights[:, :, None] * cotangent[:, None, :].astype(jnp.float32)).astype(jnp.bfloat16)
    weighted_ext = jnp.concatenate([weighted.reshape(2 * TOKENS, D), jnp.zeros((1, D), jnp.bfloat16)], axis=0)
    gate_all = jnp.transpose(w_gate.reshape(D, EXPERTS, FF), (1, 0, 2))
    up_all = jnp.transpose(w_up.reshape(D, EXPERTS, FF), (1, 0, 2))
    down_all = w_down.reshape(EXPERTS, FF, D)

    def per_expert(total, inputs):
        owner_rows, gate_w, up_w, down_w = inputs
        token_idx = (owner_rows // 2).astype(jnp.int32)
        rows_in = token_ext[token_idx]
        rows_grad = weighted_ext[owner_rows]
        gate_projection = jnp.dot(rows_in, gate_w, preferred_element_type=jnp.float32)
        up_proj = jnp.dot(rows_in, up_w, preferred_element_type=jnp.float32)
        sigmoid_gate = jax.nn.sigmoid(gate_projection)
        silu_gate = gate_projection * sigmoid_gate
        hidden = (silu_gate * up_proj).astype(jnp.bfloat16)
        grad_down_e = jnp.dot(hidden.T, rows_grad, preferred_element_type=jnp.float32).astype(jnp.bfloat16)
        grad_hidden = jnp.dot(rows_grad, down_w.T, preferred_element_type=jnp.float32)
        grad_up = (grad_hidden * silu_gate).astype(jnp.bfloat16)
        grad_gate = (grad_hidden * up_proj * sigmoid_gate * (1.0 + gate_projection * (1.0 - sigmoid_gate))).astype(jnp.bfloat16)
        count_rows = rows_in.shape[0]
        gate_blocks = grad_gate.astype(jnp.float32).reshape(count_rows, blocks, FF_DEV)
        up_blocks = grad_up.astype(jnp.float32).reshape(count_rows, blocks, FF_DEV)
        gate_w_blocks = gate_w.astype(jnp.float32).reshape(D, blocks, FF_DEV)
        up_w_blocks = up_w.astype(jnp.float32).reshape(D, blocks, FF_DEV)
        pieces = jnp.einsum("rbf,dbf->rbd", gate_blocks, gate_w_blocks, precision=lax.Precision.HIGHEST)
        pieces = pieces + jnp.einsum("rbf,dbf->rbd", up_blocks, up_w_blocks, precision=lax.Precision.HIGHEST)
        pieces = lax.optimization_barrier(pieces.astype(jnp.bfloat16))
        row_grad = jnp.sum(pieces.astype(jnp.float32), axis=1)
        total = total.at[token_idx].add(row_grad)
        return total, grad_down_e

    start = jnp.zeros((TOKENS + 1, D), jnp.float32)
    total, grad_down = lax.scan(per_expert, start, (owners, gate_all, up_all, down_all))
    return total[:TOKENS].astype(jnp.bfloat16), grad_down.reshape(EXPERTS * FF, D)
```

```python
import functools

import jax
import jax.numpy as jnp
from jax import lax
from jax.experimental import pallas as pl
from jax.experimental.pallas import tpu as pltpu
from jax.sharding import PartitionSpec as P

EXPERTS = 4
F32 = jnp.float32
BF16 = jnp.bfloat16
NT = (((1,), (1,)), ((), ()))
TN = (((0,), (0,)), ((), ()))


def matmul(a, b, dims=(((1,), (0,)), ((), ()))):
    return lax.dot_general(a, b, dims, preferred_element_type=F32)


def layer_kernel(
    n_exp, n_ten, cap, chunk,
    tok_ref, cot_ref, rw_ref, ids_ref, slot_ref, keep_ref, wg_hbm, wu_hbm, wd_hbm,
    grad_ref, hidden_ref, weighted_ref,
    wg, wu, wd, outgoing, gath, rows_in, gg, gu, piece, red, ret_out, ret_in,
    w_sem, a_send, a_recv, b_send, b_recv, c_send, c_recv, r_send, r_recv, z_send, z_recv,
):
    holders = n_exp // EXPERTS
    chips = n_ten // 2
    tok_rows, width = tok_ref.shape
    ff = wg.shape[1]
    rows = n_exp * cap
    e = lax.axis_index("expert")
    t = lax.axis_index("tensor")
    x = t // 2
    c = t % 2

    w_copies = []
    for i in range(ff // chunk):
        part = pl.ds(i * chunk, chunk)
        trio = [
            pltpu.make_async_copy(wg_hbm.at[:, part], wg.at[:, part], w_sem.at[0, i]),
            pltpu.make_async_copy(wu_hbm.at[:, part], wu.at[:, part], w_sem.at[1, i]),
            pltpu.make_async_copy(wd_hbm.at[part, :], wd.at[part, :], w_sem.at[2, i]),
        ]
        for copy in trio:
            copy.start()
        w_copies.append(trio)

    barrier = pltpu.get_barrier_semaphore()
    for k in range(1, n_exp):
        pl.semaphore_signal(
            barrier, inc=1, device_id={"expert": lax.rem(e + k, n_exp)},
            device_id_type=pl.DeviceIdType.MESH,
        )
    for k in range(1, n_ten):
        pl.semaphore_signal(
            barrier, inc=1, device_id={"tensor": lax.rem(t + k, n_ten)},
            device_id_type=pl.DeviceIdType.MESH,
        )

    ids, slot, keep = ids_ref[...], slot_ref[...], keep_ref[...]
    rw = rw_ref[...]
    target = jnp.where(keep == 1, ids * cap + slot, -1)
    row = lax.broadcasted_iota(jnp.int32, (EXPERTS * cap, tok_rows), 0)
    first, second = row == target[0:1, :], row == target[1:2, :]
    zero = jnp.zeros((), F32)
    select = (jnp.where(first, 1.0, zero) + jnp.where(second, 1.0, zero)).astype(BF16)
    row_weight = jnp.sum(
        jnp.where(first, rw[0:1, :], zero) + jnp.where(second, rw[1:2, :], zero),
        axis=1, keepdims=True,
    )
    disp = matmul(select, tok_ref[...]).astype(BF16)
    wgt = (row_weight * matmul(select, cot_ref[...])).astype(BF16)
    for i in range(EXPERTS):
        outgoing[i, 0:cap, :] = disp[i * cap : (i + 1) * cap]
        outgoing[i, cap : 2 * cap, :] = wgt[i * cap : (i + 1) * cap]
    gath[t, e] = outgoing[e // holders]
    pl.semaphore_wait(barrier, n_exp - 1 + n_ten - 1)

    def remote(src, dst, send, recv, expert, tensor):
        return pltpu.make_async_remote_copy(
            src_ref=src, dst_ref=dst, send_sem=send, recv_sem=recv,
            device_id={"expert": expert, "tensor": tensor},
            device_id_type=pl.DeviceIdType.MESH,
        )

    sent = []

    def send(*args):
        copy = remote(*args)
        copy.start()
        sent.append(copy)

    for k in range(1, n_exp):
        dest = lax.rem(e + k, n_exp)
        send(
            outgoing.at[dest // holders], gath.at[t, e], a_send.at[k], a_recv.at[k], dest, t
        )
    mate = x * 2 + (1 - c)
    for k in range(n_exp):
        s = lax.rem(e - k + n_exp, n_exp)
        block = gath.at[t, s]
        if k:
            remote(block, block, a_send.at[k], a_recv.at[k], s, t).wait_recv()
        for dx in range(1, chips):
            send(
                block, block, b_send.at[dx, k], b_recv.at[dx, k], e,
                lax.rem(x + dx, chips) * 2 + c,
            )
        send(block, block, b_send.at[0, k], b_recv.at[0, k], e, mate)
    for k in range(n_exp):
        s = lax.rem(e - k + n_exp, n_exp)
        for dx in range(1, chips):
            block = gath.at[lax.rem(x - dx + chips, chips) * 2 + c, s]
            remote(
                block, block, b_send.at[dx, k], b_recv.at[dx, k], e, mate
            ).wait_recv()
            send(block, block, c_send.at[dx, k], c_recv.at[dx, k], e, mate)
    for k in range(n_exp):
        s = lax.rem(e - k + n_exp, n_exp)
        block = gath.at[mate, s]
        remote(block, block, b_send.at[0, k], b_recv.at[0, k], e, mate).wait_recv()
        for dx in range(1, chips):
            block = gath.at[lax.rem(x - dx + chips, chips) * 2 + (1 - c), s]
            remote(block, block, c_send.at[dx, k], c_recv.at[dx, k], e, mate).wait_recv()
    for j in range(n_ten):
        for s in range(n_exp):
            place = (slice(s * cap, (s + 1) * cap), slice(j * width, (j + 1) * width))
            rows_in[place] = gath[j, s, 0:cap, :]
            weighted_ref[place] = gath[j, s, cap : 2 * cap, :]

    for i in range(ff // chunk):
        part = slice(i * chunk, (i + 1) * chunk)
        w_copies[i][0].wait()
        w_copies[i][1].wait()
        w_copies[i][2].wait()
        gate = matmul(rows_in[...], wg[:, part])
        up = matmul(rows_in[...], wu[:, part])
        back = matmul(weighted_ref[...], wd[part, :], NT)
        sigmoid = jax.nn.sigmoid(gate)
        silu = gate * sigmoid
        hidden_ref[:, part] = (silu * up).astype(BF16)
        gu[:, part] = (back * silu).astype(BF16)
        gg[:, part] = (back * up * sigmoid * (1.0 + gate * (1.0 - sigmoid))).astype(BF16)

    order = [(dx, dc) for dx in range(1, chips) for dc in range(2)] + [(0, 1), (0, 0)]
    for j, (dx, dc) in enumerate(order):
        dest = lax.rem(x + dx, chips) * 2 + (c if dc == 0 else 1 - c)
        part = pl.ds(pl.multiple_of(dest * width, width), width)
        value = matmul(gg[...], wg[part, :], NT) + matmul(gu[...], wu[part, :], NT)
        piece[j] = value.astype(BF16)
        if j < n_ten - 1:
            send(piece.at[j], red.at[j], r_send.at[j], r_recv.at[j], e, dest)
    total = piece[n_ten - 1].astype(F32)
    for j in range(n_ten - 1):
        remote(piece.at[j], red.at[j], r_send.at[j], r_recv.at[j], e, mate).wait_recv()
        total = total + red[j].astype(F32)
    ret_out[...] = total.astype(BF16).reshape(n_exp, cap, width)
    for k in range(1, n_exp):
        dest = lax.rem(e + k, n_exp)
        send(ret_out.at[dest], ret_in.at[e], z_send.at[k], z_recv.at[k], dest, t)
    ret_in[e] = ret_out[e]
    for k in range(1, n_exp):
        s = lax.rem(e - k + n_exp, n_exp)
        remote(ret_out.at[s], ret_in.at[s], z_send.at[k], z_recv.at[k], s, t).wait_recv()

    row = lax.broadcasted_iota(jnp.int32, (rows, tok_rows), 0)
    owner = row >> ((cap * holders).bit_length() - 1)
    row = owner * cap + (row & (cap - 1))
    first, second = row == target[0:1, :], row == target[1:2, :]
    select = (jnp.where(first, 1.0, zero) + jnp.where(second, 1.0, zero)).astype(BF16)
    grad_ref[...] = matmul(select, ret_in[...].reshape(rows, width), TN).astype(BF16)
    for copy in sent:
        copy.wait_send()


def shards(
    tokens, cotangent, route_weights, expert_ids, slot_index, keep_mask, w_gate, w_up, w_down
):
    tok_rows, width = tokens.shape
    cap = tok_rows // 2
    n_exp, n_ten = lax.axis_size("expert"), lax.axis_size("tensor")
    chips = n_ten // 2
    rows = n_exp * cap
    depth, ff = w_gate.shape
    chunk = min(512, ff)
    dma = pltpu.SemaphoreType.DMA
    vmem = pl.BlockSpec(memory_space=pltpu.VMEM)
    hbm = pl.BlockSpec(memory_space=pl.ANY)
    grad_tokens, hidden, weighted = pl.pallas_call(
        functools.partial(layer_kernel, n_exp, n_ten, cap, chunk),
        out_shape=(
            jax.ShapeDtypeStruct((tok_rows, width), BF16),
            jax.ShapeDtypeStruct((rows, ff), BF16),
            jax.ShapeDtypeStruct((rows, depth), BF16),
        ),
        in_specs=[vmem] * 6 + [hbm] * 3,
        out_specs=(vmem, vmem, vmem),
        scratch_shapes=[
            pltpu.VMEM((depth, ff), BF16),
            pltpu.VMEM((depth, ff), BF16),
            pltpu.VMEM((ff, depth), BF16),
            pltpu.VMEM((EXPERTS, 2 * cap, width), BF16),
            pltpu.VMEM((n_ten, n_exp, 2 * cap, width), BF16),
            pltpu.VMEM((rows, depth), BF16),
            pltpu.VMEM((rows, ff), BF16),
            pltpu.VMEM((rows, ff), BF16),
            pltpu.VMEM((n_ten, rows, width), BF16),
            pltpu.VMEM((n_ten, rows, width), BF16),
            pltpu.VMEM((n_exp, cap, width), BF16),
            pltpu.VMEM((n_exp, cap, width), BF16),
            dma((3, ff // chunk)),
            dma((n_exp,)),
            dma((n_exp,)),
            dma((chips, n_exp)),
            dma((chips, n_exp)),
            dma((chips, n_exp)),
            dma((chips, n_exp)),
            dma((n_ten,)),
            dma((n_ten,)),
            dma((n_exp,)),
            dma((n_exp,)),
        ],
        compiler_params=pltpu.CompilerParams(
            collective_id=0, has_side_effects=True, vmem_limit_bytes=56 * 2**20
        ),
        cost_estimate=pl.CostEstimate(
            flops=10 * rows * depth * ff,
            bytes_accessed=6 * depth * ff,
            transcendentals=rows * ff,
        ),
    )(
        tokens, cotangent, route_weights.T, expert_ids.T, slot_index.T, keep_mask.T,
        w_gate, w_up, w_down,
    )
    grad_down = lax.dot_general(hidden, weighted, TN, preferred_element_type=F32).astype(BF16)
    return grad_tokens, grad_down


def solution(mesh):
    in_specs = (
        P(("groups", "expert"), "tensor"),
        P(("groups", "expert"), "tensor"),
        P(("groups", "expert"), None),
        P(("groups", "expert"), None),
        P(("groups", "expert"), None),
        P(("groups", "expert"), None),
        P(None, ("expert", "tensor")),
        P(None, ("expert", "tensor")),
        P(("expert", "tensor"), None),
    )
    out_specs = (P(("groups", "expert"), "tensor"), P(("groups", "expert", "tensor"), None))
    return jax.shard_map(shards, mesh=mesh, in_specs=in_specs, out_specs=out_specs, check_vma=False)
```

```python
import functools

import jax
import jax.numpy as jnp
from jax import lax
from jax.experimental import pallas as pl
from jax.experimental.pallas import tpu as pltpu
from jax.sharding import PartitionSpec as P

EXPERTS = 4
F32 = jnp.float32
BF16 = jnp.bfloat16
NT = (((1,), (1,)), ((), ()))
TN = (((0,), (0,)), ((), ()))


def matmul(a, b, dims=(((1,), (0,)), ((), ()))):
    return lax.dot_general(a, b, dims, preferred_element_type=F32)


def layer_kernel(
    n_exp, n_ten, cap, chunk,
    tok_ref, cot_ref, rw_ref, ids_ref, slot_ref, keep_ref, wg_hbm, wu_hbm, wd_hbm,
    ret_ref, hidden_ref, weighted_ref,
    wg, wu, wd, outgoing, gath, gate_acc, up_acc, back_acc, gg, gu, piece, red, ret_out, ret_in,
    w_sem, a_send, a_recv, b_send, b_recv, c_send, c_recv, r_send, r_recv, z_send, z_recv,
):
    holders = n_exp // EXPERTS
    chips = n_ten // 2
    tok_rows, width = tok_ref.shape
    ff = wg.shape[1]
    rows = n_exp * cap
    e = lax.axis_index("expert")
    t = lax.axis_index("tensor")
    x = t // 2
    c = t % 2

    arrivals = [(dx, dc) for dx in range(chips) for dc in range(2)]
    blocks = [
        lax.rem(x - dx + chips, chips) * 2 + (c if dc == 0 else 1 - c) for dx, dc in arrivals
    ]
    w_copies = []
    for i, block in enumerate(blocks):
        part = pl.ds(pl.multiple_of(block * width, width), width)
        trio = [
            pltpu.make_async_copy(wg_hbm.at[part, :], wg.at[part, :], w_sem.at[0, i]),
            pltpu.make_async_copy(wu_hbm.at[part, :], wu.at[part, :], w_sem.at[1, i]),
            pltpu.make_async_copy(wd_hbm.at[:, part], wd.at[:, part], w_sem.at[2, i]),
        ]
        for copy in trio:
            copy.start()
        w_copies.append(trio)

    barrier = pltpu.get_barrier_semaphore()
    for k in range(1, n_exp):
        pl.semaphore_signal(
            barrier, inc=1, device_id={"expert": lax.rem(e + k, n_exp)},
            device_id_type=pl.DeviceIdType.MESH,
        )
    for k in range(1, n_ten):
        pl.semaphore_signal(
            barrier, inc=1, device_id={"tensor": lax.rem(t + k, n_ten)},
            device_id_type=pl.DeviceIdType.MESH,
        )

    ids, slot, keep = ids_ref[...], slot_ref[...], keep_ref[...]
    rw = rw_ref[...]
    target = jnp.where(keep == 1, ids * cap + slot, -1)
    row = lax.broadcasted_iota(jnp.int32, (EXPERTS * cap, tok_rows), 0)
    first, second = row == target[0:1, :], row == target[1:2, :]
    zero = jnp.zeros((), F32)
    select = (jnp.where(first, 1.0, zero) + jnp.where(second, 1.0, zero)).astype(BF16)
    row_weight = jnp.sum(
        jnp.where(first, rw[0:1, :], zero) + jnp.where(second, rw[1:2, :], zero),
        axis=1, keepdims=True,
    )
    disp = matmul(select, tok_ref[...]).astype(BF16)
    wgt = (row_weight * matmul(select, cot_ref[...])).astype(BF16)
    for i in range(EXPERTS):
        outgoing[i, 0:cap, :] = disp[i * cap : (i + 1) * cap]
        outgoing[i, cap : 2 * cap, :] = wgt[i * cap : (i + 1) * cap]
    gath[t, e] = outgoing[e // holders]
    pl.semaphore_wait(barrier, n_exp - 1 + n_ten - 1)

    def remote(src, dst, send, recv, expert, tensor):
        return pltpu.make_async_remote_copy(
            src_ref=src, dst_ref=dst, send_sem=send, recv_sem=recv,
            device_id={"expert": expert, "tensor": tensor},
            device_id_type=pl.DeviceIdType.MESH,
        )

    sent = []

    def send(*args):
        copy = remote(*args)
        copy.start()
        sent.append(copy)

    for k in range(1, n_exp):
        dest = lax.rem(e + k, n_exp)
        send(
            outgoing.at[dest // holders], gath.at[t, e], a_send.at[k], a_recv.at[k], dest, t
        )
    mate = x * 2 + (1 - c)
    for k in range(n_exp):
        s = lax.rem(e - k + n_exp, n_exp)
        block = gath.at[t, s]
        if k:
            remote(block, block, a_send.at[k], a_recv.at[k], s, t).wait_recv()
        for dx in range(1, chips):
            send(
                block, block, b_send.at[dx, k], b_recv.at[dx, k], e,
                lax.rem(x + dx, chips) * 2 + c,
            )
        send(block, block, b_send.at[0, k], b_recv.at[0, k], e, mate)

    def project(i):
        for copy in w_copies[i]:
            copy.wait()
        part = pl.ds(pl.multiple_of(blocks[i] * width, width), width)
        both = gath[blocks[i]]
        rows_in = both[:, 0:cap, :].reshape(rows, width)
        weighted = both[:, cap : 2 * cap, :].reshape(rows, width)
        weighted_ref[:, part] = weighted
        for j in range(ff // chunk):
            cols = slice(j * chunk, (j + 1) * chunk)
            gate = matmul(rows_in, wg[part, cols])
            up = matmul(rows_in, wu[part, cols])
            back = matmul(weighted, wd[cols, part], NT)
            if i:
                gate = gate + gate_acc[:, cols]
                up = up + up_acc[:, cols]
                back = back + back_acc[:, cols]
            if i < n_ten - 1:
                gate_acc[:, cols] = gate
                up_acc[:, cols] = up
                back_acc[:, cols] = back
            else:
                sigmoid = jax.nn.sigmoid(gate)
                silu = gate * sigmoid
                hidden_ref[:, cols] = (silu * up).astype(BF16)
                gu[:, cols] = (back * silu).astype(BF16)
                gg[:, cols] = (back * up * sigmoid * (1.0 + gate * (1.0 - sigmoid))).astype(BF16)

    project(0)
    for k in range(n_exp):
        s = lax.rem(e - k + n_exp, n_exp)
        for dx in range(1, chips):
            block = gath.at[blocks[2 * dx], s]
            remote(
                block, block, b_send.at[dx, k], b_recv.at[dx, k], e, mate
            ).wait_recv()
            send(block, block, c_send.at[dx, k], c_recv.at[dx, k], e, mate)
    for k in range(n_exp):
        s = lax.rem(e - k + n_exp, n_exp)
        block = gath.at[mate, s]
        remote(block, block, b_send.at[0, k], b_recv.at[0, k], e, mate).wait_recv()
    project(1)
    for dx in range(1, chips):
        project(2 * dx)
        for k in range(n_exp):
            s = lax.rem(e - k + n_exp, n_exp)
            block = gath.at[blocks[2 * dx + 1], s]
            remote(block, block, c_send.at[dx, k], c_recv.at[dx, k], e, mate).wait_recv()
        project(2 * dx + 1)

    order = [(dx, dc) for dx in range(1, chips) for dc in range(2)] + [(0, 1), (0, 0)]
    for j, (dx, dc) in enumerate(order):
        dest = lax.rem(x + dx, chips) * 2 + (c if dc == 0 else 1 - c)
        part = pl.ds(pl.multiple_of(dest * width, width), width)
        value = matmul(gg[...], wg[part, :], NT) + matmul(gu[...], wu[part, :], NT)
        piece[j] = value.astype(BF16)
        if j < n_ten - 1:
            send(piece.at[j], red.at[j], r_send.at[j], r_recv.at[j], e, dest)
    total = piece[n_ten - 1].astype(F32)
    for j in range(n_ten - 1):
        remote(piece.at[j], red.at[j], r_send.at[j], r_recv.at[j], e, mate).wait_recv()
        total = total + red[j].astype(F32)
    ret_out[...] = total.astype(BF16).reshape(n_exp, cap, width)
    for k in range(1, n_exp):
        dest = lax.rem(e + k, n_exp)
        send(ret_out.at[dest], ret_in.at[e], z_send.at[k], z_recv.at[k], dest, t)
    ret_in[e] = ret_out[e]
    for k in range(1, n_exp):
        s = lax.rem(e - k + n_exp, n_exp)
        remote(ret_out.at[s], ret_in.at[s], z_send.at[k], z_recv.at[k], s, t).wait_recv()

    ret_ref[...] = ret_in[...]
    for copy in sent:
        copy.wait_send()


def down_kernel(
    cap, holders, ids_ref, slot_ref, keep_ref, ret_ref, hidden_ref, weighted_ref,
    grad_ref, out_ref,
):
    out_ref[...] = matmul(hidden_ref[...], weighted_ref[...], TN).astype(BF16)

    @pl.when(pl.program_id(0) == 0)
    def _():
        n_exp, _, width = ret_ref.shape
        rows = n_exp * cap
        target = jnp.where(keep_ref[...] == 1, ids_ref[...] * cap + slot_ref[...], -1)
        row = lax.broadcasted_iota(jnp.int32, (rows, target.shape[1]), 0)
        owner = row >> ((cap * holders).bit_length() - 1)
        row = owner * cap + (row & (cap - 1))
        first, second = row == target[0:1, :], row == target[1:2, :]
        zero = jnp.zeros((), F32)
        select = (jnp.where(first, 1.0, zero) + jnp.where(second, 1.0, zero)).astype(BF16)
        grad_ref[...] = matmul(select, ret_ref[...].reshape(rows, width), TN).astype(BF16)


def shards(
    tokens, cotangent, route_weights, expert_ids, slot_index, keep_mask, w_gate, w_up, w_down
):
    tok_rows, width = tokens.shape
    cap = tok_rows // 2
    n_exp, n_ten = lax.axis_size("expert"), lax.axis_size("tensor")
    chips = n_ten // 2
    rows = n_exp * cap
    depth, ff = w_gate.shape
    chunk = min(512, ff)
    meta = (expert_ids.T, slot_index.T, keep_mask.T)
    dma = pltpu.SemaphoreType.DMA
    vmem = pl.BlockSpec(memory_space=pltpu.VMEM)
    hbm = pl.BlockSpec(memory_space=pl.ANY)
    returned, hidden, weighted = pl.pallas_call(
        functools.partial(layer_kernel, n_exp, n_ten, cap, chunk),
        out_shape=(
            jax.ShapeDtypeStruct((n_exp, cap, width), BF16),
            jax.ShapeDtypeStruct((rows, ff), BF16),
            jax.ShapeDtypeStruct((rows, depth), BF16),
        ),
        in_specs=[vmem] * 6 + [hbm] * 3,
        out_specs=(vmem, vmem, vmem),
        scratch_shapes=[
            pltpu.VMEM((depth, ff), BF16),
            pltpu.VMEM((depth, ff), BF16),
            pltpu.VMEM((ff, depth), BF16),
            pltpu.VMEM((EXPERTS, 2 * cap, width), BF16),
            pltpu.VMEM((n_ten, n_exp, 2 * cap, width), BF16),
            pltpu.VMEM((rows, ff), F32),
            pltpu.VMEM((rows, ff), F32),
            pltpu.VMEM((rows, ff), F32),
            pltpu.VMEM((rows, ff), BF16),
            pltpu.VMEM((rows, ff), BF16),
            pltpu.VMEM((n_ten, rows, width), BF16),
            pltpu.VMEM((n_ten, rows, width), BF16),
            pltpu.VMEM((n_exp, cap, width), BF16),
            pltpu.VMEM((n_exp, cap, width), BF16),
            dma((3, n_ten)),
            dma((n_exp,)),
            dma((n_exp,)),
            dma((chips, n_exp)),
            dma((chips, n_exp)),
            dma((chips, n_exp)),
            dma((chips, n_exp)),
            dma((n_ten,)),
            dma((n_ten,)),
            dma((n_exp,)),
            dma((n_exp,)),
        ],
        compiler_params=pltpu.CompilerParams(
            collective_id=0, has_side_effects=True, vmem_limit_bytes=56 * 2**20
        ),
        cost_estimate=pl.CostEstimate(
            flops=10 * rows * depth * ff,
            bytes_accessed=6 * depth * ff,
            transcendentals=rows * ff,
        ),
    )(
        tokens, cotangent, route_weights.T, *meta,
        w_gate, w_up, w_down,
    )
    tile = min(512, ff)
    grad_tokens, grad_down = pl.pallas_call(
        functools.partial(down_kernel, cap, n_exp // EXPERTS),
        out_shape=(
            jax.ShapeDtypeStruct((tok_rows, width), BF16),
            jax.ShapeDtypeStruct((ff, depth), BF16),
        ),
        grid=(ff // tile,),
        in_specs=[pl.BlockSpec((2, tok_rows), lambda i: (0, 0))] * 3
        + [
            pl.BlockSpec((n_exp, cap, width), lambda i: (0, 0, 0)),
            pl.BlockSpec((rows, tile), lambda i: (0, i)),
            pl.BlockSpec((rows, depth), lambda i: (0, 0)),
        ],
        out_specs=(
            pl.BlockSpec((tok_rows, width), lambda i: (0, 0)),
            pl.BlockSpec((tile, depth), lambda i: (i, 0)),
        ),
        compiler_params=pltpu.CompilerParams(vmem_limit_bytes=32 * 2**20),
        cost_estimate=pl.CostEstimate(
            flops=2 * rows * depth * ff, bytes_accessed=2 * depth * ff, transcendentals=0
        ),
    )(*meta, returned, hidden, weighted)
    return grad_tokens, grad_down


def solution(mesh):
    in_specs = (
        P(("groups", "expert"), "tensor"),
        P(("groups", "expert"), "tensor"),
        P(("groups", "expert"), None),
        P(("groups", "expert"), None),
        P(("groups", "expert"), None),
        P(("groups", "expert"), None),
        P(None, ("expert", "tensor")),
        P(None, ("expert", "tensor")),
        P(("expert", "tensor"), None),
    )
    out_specs = (P(("groups", "expert"), "tensor"), P(("groups", "expert", "tensor"), None))
    return jax.shard_map(shards, mesh=mesh, in_specs=in_specs, out_specs=out_specs, check_vma=False)
```

```python
import functools

import jax
import jax.numpy as jnp
from jax import lax
from jax.experimental import pallas as pl
from jax.experimental.pallas import tpu as pltpu
from jax.sharding import PartitionSpec as P

EXPERTS = 4
F32 = jnp.float32
BF16 = jnp.bfloat16
NT = (((1,), (1,)), ((), ()))
TN = (((0,), (0,)), ((), ()))


def matmul(a, b, dims=(((1,), (0,)), ((), ()))):
    return lax.dot_general(a, b, dims, preferred_element_type=F32)


def layer_kernel(
    n_exp, n_ten, cap, chunk,
    tok_ref, cot_ref, rw_ref, ids_ref, slot_ref, keep_ref, wg_hbm, wu_hbm, wd_hbm,
    ret_ref, hidden_out, weighted_out,
    hidden_ref, weighted_ref, wg, wu, wd, outgoing, gath, gate_acc, up_acc, back_acc, gg, gu, piece, red, ret_out, ret_in,
    w_sem, o_sem, a_send, a_recv, b_send, b_recv, c_send, c_recv, r_send, r_recv, z_send, z_recv,
):
    holders = n_exp // EXPERTS
    chips = n_ten // 2
    tok_rows, width = tok_ref.shape
    ff = wg.shape[1]
    rows = n_exp * cap
    e = lax.axis_index("expert")
    t = lax.axis_index("tensor")
    x = t // 2
    c = t % 2

    arrivals = [(dx, dc) for dx in range(chips) for dc in range(2)]
    blocks = [
        lax.rem(x - dx + chips, chips) * 2 + (c if dc == 0 else 1 - c) for dx, dc in arrivals
    ]
    w_copies = []
    for i, block in enumerate(blocks):
        part = pl.ds(pl.multiple_of(block * width, width), width)
        trio = [
            pltpu.make_async_copy(wg_hbm.at[part, :], wg.at[part, :], w_sem.at[0, i]),
            pltpu.make_async_copy(wu_hbm.at[part, :], wu.at[part, :], w_sem.at[1, i]),
            pltpu.make_async_copy(wd_hbm.at[:, part], wd.at[:, part], w_sem.at[2, i]),
        ]
        for copy in trio:
            copy.start()
        w_copies.append(trio)

    barrier = pltpu.get_barrier_semaphore()
    for k in range(1, n_exp):
        pl.semaphore_signal(
            barrier, inc=1, device_id={"expert": lax.rem(e + k, n_exp)},
            device_id_type=pl.DeviceIdType.MESH,
        )
    for k in range(1, n_ten):
        pl.semaphore_signal(
            barrier, inc=1, device_id={"tensor": lax.rem(t + k, n_ten)},
            device_id_type=pl.DeviceIdType.MESH,
        )

    ids, slot, keep = ids_ref[...], slot_ref[...], keep_ref[...]
    rw = rw_ref[...]
    target = jnp.where(keep == 1, ids * cap + slot, -1)
    row = lax.broadcasted_iota(jnp.int32, (EXPERTS * cap, tok_rows), 0)
    first, second = row == target[0:1, :], row == target[1:2, :]
    zero = jnp.zeros((), F32)
    select = (jnp.where(first, 1.0, zero) + jnp.where(second, 1.0, zero)).astype(BF16)
    row_weight = jnp.sum(
        jnp.where(first, rw[0:1, :], zero) + jnp.where(second, rw[1:2, :], zero),
        axis=1, keepdims=True,
    )
    disp = matmul(select, tok_ref[...]).astype(BF16)
    wgt = (row_weight * matmul(select, cot_ref[...])).astype(BF16)
    for i in range(EXPERTS):
        outgoing[i, 0:cap, :] = disp[i * cap : (i + 1) * cap]
        outgoing[i, cap : 2 * cap, :] = wgt[i * cap : (i + 1) * cap]
    gath[t, e] = outgoing[e // holders]
    pl.semaphore_wait(barrier, n_exp - 1 + n_ten - 1)

    def remote(src, dst, send, recv, expert, tensor):
        return pltpu.make_async_remote_copy(
            src_ref=src, dst_ref=dst, send_sem=send, recv_sem=recv,
            device_id={"expert": expert, "tensor": tensor},
            device_id_type=pl.DeviceIdType.MESH,
        )

    sent = []

    def send(*args):
        copy = remote(*args)
        copy.start()
        sent.append(copy)

    for k in range(1, n_exp):
        dest = lax.rem(e + k, n_exp)
        send(
            outgoing.at[dest // holders], gath.at[t, e], a_send.at[k], a_recv.at[k], dest, t
        )
    mate = x * 2 + (1 - c)
    for k in range(n_exp):
        s = lax.rem(e - k + n_exp, n_exp)
        block = gath.at[t, s]
        if k:
            remote(block, block, a_send.at[k], a_recv.at[k], s, t).wait_recv()
        for dx in range(1, chips):
            send(
                block, block, b_send.at[dx, k], b_recv.at[dx, k], e,
                lax.rem(x + dx, chips) * 2 + c,
            )
        send(block, block, b_send.at[0, k], b_recv.at[0, k], e, mate)

    def project(i):
        for copy in w_copies[i]:
            copy.wait()
        part = pl.ds(pl.multiple_of(blocks[i] * width, width), width)
        both = gath[blocks[i]]
        rows_in = both[:, 0:cap, :].reshape(rows, width)
        weighted = both[:, cap : 2 * cap, :].reshape(rows, width)
        weighted_ref[:, part] = weighted
        for j in range(ff // chunk):
            cols = slice(j * chunk, (j + 1) * chunk)
            gate = matmul(rows_in, wg[part, cols])
            up = matmul(rows_in, wu[part, cols])
            back = matmul(weighted, wd[cols, part], NT)
            if i:
                gate = gate + gate_acc[:, cols]
                up = up + up_acc[:, cols]
                back = back + back_acc[:, cols]
            if i < n_ten - 1:
                gate_acc[:, cols] = gate
                up_acc[:, cols] = up
                back_acc[:, cols] = back
            else:
                sigmoid = jax.nn.sigmoid(gate)
                silu = gate * sigmoid
                hidden_ref[:, cols] = (silu * up).astype(BF16)
                gu[:, cols] = (back * silu).astype(BF16)
                gg[:, cols] = (back * up * sigmoid * (1.0 + gate * (1.0 - sigmoid))).astype(BF16)

    project(0)
    for k in range(n_exp):
        s = lax.rem(e - k + n_exp, n_exp)
        for dx in range(1, chips):
            block = gath.at[blocks[2 * dx], s]
            remote(
                block, block, b_send.at[dx, k], b_recv.at[dx, k], e, mate
            ).wait_recv()
            send(block, block, c_send.at[dx, k], c_recv.at[dx, k], e, mate)
    for k in range(n_exp):
        s = lax.rem(e - k + n_exp, n_exp)
        block = gath.at[mate, s]
        remote(block, block, b_send.at[0, k], b_recv.at[0, k], e, mate).wait_recv()
    project(1)
    for dx in range(1, chips):
        project(2 * dx)
        for k in range(n_exp):
            s = lax.rem(e - k + n_exp, n_exp)
            block = gath.at[blocks[2 * dx + 1], s]
            remote(block, block, c_send.at[dx, k], c_recv.at[dx, k], e, mate).wait_recv()
        project(2 * dx + 1)
    out_copies = [
        pltpu.make_async_copy(hidden_ref, hidden_out, o_sem.at[0]),
        pltpu.make_async_copy(weighted_ref, weighted_out, o_sem.at[1]),
    ]
    for copy in out_copies:
        copy.start()

    order = [(dx, dc) for dx in range(1, chips) for dc in range(2)] + [(0, 1), (0, 0)]
    for j, (dx, dc) in enumerate(order):
        dest = lax.rem(x + dx, chips) * 2 + (c if dc == 0 else 1 - c)
        part = pl.ds(pl.multiple_of(dest * width, width), width)
        value = matmul(gg[...], wg[part, :], NT) + matmul(gu[...], wu[part, :], NT)
        piece[j] = value.astype(BF16)
        if j < n_ten - 1:
            send(piece.at[j], red.at[j], r_send.at[j], r_recv.at[j], e, dest)
    total = piece[n_ten - 1].astype(F32)
    for j in range(n_ten - 1):
        remote(piece.at[j], red.at[j], r_send.at[j], r_recv.at[j], e, mate).wait_recv()
        total = total + red[j].astype(F32)
    ret_out[...] = total.astype(BF16).reshape(n_exp, cap, width)
    for k in range(1, n_exp):
        dest = lax.rem(e + k, n_exp)
        send(ret_out.at[dest], ret_in.at[e], z_send.at[k], z_recv.at[k], dest, t)
    ret_in[e] = ret_out[e]
    for k in range(1, n_exp):
        s = lax.rem(e - k + n_exp, n_exp)
        remote(ret_out.at[s], ret_in.at[s], z_send.at[k], z_recv.at[k], s, t).wait_recv()

    ret_ref[...] = ret_in[...]
    for copy in sent:
        copy.wait_send()
    for copy in out_copies:
        copy.wait()


def down_kernel(
    cap, holders, ids_ref, slot_ref, keep_ref, ret_ref, hidden_ref, weighted_ref,
    grad_ref, out_ref,
):
    out_ref[...] = matmul(hidden_ref[...], weighted_ref[...], TN).astype(BF16)

    @pl.when(pl.program_id(0) == 0)
    def _():
        n_exp, _, width = ret_ref.shape
        rows = n_exp * cap
        target = jnp.where(keep_ref[...] == 1, ids_ref[...] * cap + slot_ref[...], -1)
        row = lax.broadcasted_iota(jnp.int32, (rows, target.shape[1]), 0)
        owner = row >> ((cap * holders).bit_length() - 1)
        row = owner * cap + (row & (cap - 1))
        first, second = row == target[0:1, :], row == target[1:2, :]
        zero = jnp.zeros((), F32)
        select = (jnp.where(first, 1.0, zero) + jnp.where(second, 1.0, zero)).astype(BF16)
        grad_ref[...] = matmul(select, ret_ref[...].reshape(rows, width), TN).astype(BF16)


def shards(
    tokens, cotangent, route_weights, expert_ids, slot_index, keep_mask, w_gate, w_up, w_down
):
    tok_rows, width = tokens.shape
    cap = tok_rows // 2
    n_exp, n_ten = lax.axis_size("expert"), lax.axis_size("tensor")
    chips = n_ten // 2
    rows = n_exp * cap
    depth, ff = w_gate.shape
    chunk = min(512, ff)
    meta = (expert_ids.T, slot_index.T, keep_mask.T)
    dma = pltpu.SemaphoreType.DMA
    vmem = pl.BlockSpec(memory_space=pltpu.VMEM)
    hbm = pl.BlockSpec(memory_space=pl.ANY)
    returned, hidden, weighted = pl.pallas_call(
        functools.partial(layer_kernel, n_exp, n_ten, cap, chunk),
        out_shape=(
            jax.ShapeDtypeStruct((n_exp, cap, width), BF16),
            jax.ShapeDtypeStruct((rows, ff), BF16),
            jax.ShapeDtypeStruct((rows, depth), BF16),
        ),
        in_specs=[vmem] * 6 + [hbm] * 3,
        out_specs=(vmem, hbm, hbm),
        scratch_shapes=[
            pltpu.VMEM((rows, ff), BF16),
            pltpu.VMEM((rows, depth), BF16),
            pltpu.VMEM((depth, ff), BF16),
            pltpu.VMEM((depth, ff), BF16),
            pltpu.VMEM((ff, depth), BF16),
            pltpu.VMEM((EXPERTS, 2 * cap, width), BF16),
            pltpu.VMEM((n_ten, n_exp, 2 * cap, width), BF16),
            pltpu.VMEM((rows, ff), F32),
            pltpu.VMEM((rows, ff), F32),
            pltpu.VMEM((rows, ff), F32),
            pltpu.VMEM((rows, ff), BF16),
            pltpu.VMEM((rows, ff), BF16),
            pltpu.VMEM((n_ten, rows, width), BF16),
            pltpu.VMEM((n_ten, rows, width), BF16),
            pltpu.VMEM((n_exp, cap, width), BF16),
            pltpu.VMEM((n_exp, cap, width), BF16),
            dma((3, n_ten)),
            dma((2,)),
            dma((n_exp,)),
            dma((n_exp,)),
            dma((chips, n_exp)),
            dma((chips, n_exp)),
            dma((chips, n_exp)),
            dma((chips, n_exp)),
            dma((n_ten,)),
            dma((n_ten,)),
            dma((n_exp,)),
            dma((n_exp,)),
        ],
        compiler_params=pltpu.CompilerParams(
            collective_id=0, has_side_effects=True, vmem_limit_bytes=56 * 2**20
        ),
        cost_estimate=pl.CostEstimate(
            flops=10 * rows * depth * ff,
            bytes_accessed=6 * depth * ff,
            transcendentals=rows * ff,
        ),
    )(
        tokens, cotangent, route_weights.T, *meta,
        w_gate, w_up, w_down,
    )
    tile = min(512, ff)
    grad_tokens, grad_down = pl.pallas_call(
        functools.partial(down_kernel, cap, n_exp // EXPERTS),
        out_shape=(
            jax.ShapeDtypeStruct((tok_rows, width), BF16),
            jax.ShapeDtypeStruct((ff, depth), BF16),
        ),
        grid=(ff // tile,),
        in_specs=[pl.BlockSpec((2, tok_rows), lambda i: (0, 0))] * 3
        + [
            pl.BlockSpec((n_exp, cap, width), lambda i: (0, 0, 0)),
            pl.BlockSpec((rows, tile), lambda i: (0, i)),
            pl.BlockSpec((rows, depth), lambda i: (0, 0)),
        ],
        out_specs=(
            pl.BlockSpec((tok_rows, width), lambda i: (0, 0)),
            pl.BlockSpec((tile, depth), lambda i: (i, 0)),
        ),
        compiler_params=pltpu.CompilerParams(vmem_limit_bytes=56 * 2**20),
        cost_estimate=pl.CostEstimate(
            flops=2 * rows * depth * ff, bytes_accessed=2 * depth * ff, transcendentals=0
        ),
    )(*meta, returned, hidden, weighted)
    return grad_tokens, grad_down


def solution(mesh):
    in_specs = (
        P(("groups", "expert"), "tensor"),
        P(("groups", "expert"), "tensor"),
        P(("groups", "expert"), None),
        P(("groups", "expert"), None),
        P(("groups", "expert"), None),
        P(("groups", "expert"), None),
        P(None, ("expert", "tensor")),
        P(None, ("expert", "tensor")),
        P(("expert", "tensor"), None),
    )
    out_specs = (P(("groups", "expert"), "tensor"), P(("groups", "expert", "tensor"), None))
    return jax.shard_map(shards, mesh=mesh, in_specs=in_specs, out_specs=out_specs, check_vma=False)
```
